256 devices in a mesh: dp: 32 (over z_lo, y, core), tensor: 8 (over z_hi, x).
Axes of the slice: x: 4, y: 4, z: 8 (z_hi: 2, z_lo: 4; z = z_hi * 4 + z_lo), core: 2. Of those that a mesh axis runs over, the one named last changes fastest.
Arguments:
- activations: bfloat16 [32768, 4096], P('dp', 'tensor'), may hold values from -6 to 6
- grad_out: bfloat16 [32768, 11008], P('dp', 'tensor'), may hold values from -0.049804688 to 0.049804688
- subspace: bfloat16 [4096, 512], replicated, may hold values from -0.09375 to 0.09375
- first_moment: float32 [512, 11008], P('dp', 'tensor'), may hold values from -2 to 2
- second_moment: float32 [512, 11008], P('dp', 'tensor'), may hold values from 0.0001 to 0.001
Outputs:
- update: bfloat16 [4096, 11008], P('dp', 'tensor')
- new_first: float32 [512, 11008], P('dp', 'tensor')
- new_second: float32 [512, 11008], P('dp', 'tensor')
The draws below stay inside these ranges and needn't reach their ends.
All inputs are finite; a program needn't handle non-finite values.
Results may differ from the reference program's by a relative error of at most 0.006.
Values may be sent and summed in bfloat16 or wider, within the bound.
A program may use at most 64 MiB of HBM per device.

```python
import math
import jax
import jax.numpy as jnp
from jax import lax

D = 4096
FF = 11008
RANK = 512
STEP = 10
TOKENS = 32768


def shard_levels(stream_key, dims, cuts, low, top_value):
    factor_of = 1.0
    for dim, blocks in cuts:
        draws = jax.random.uniform(jax.random.fold_in(jax.random.fold_in(stream_key, 6), dim), (blocks,), jnp.float32, low / len(cuts), top_value / len(cuts))
        factor_of = factor_of * jnp.repeat(jnp.exp(draws), dims[dim] // blocks).reshape((-1,) + (1,) * (len(dims) - 1 - dim))
    return factor_of


def scatter_about(own_key, shape, spread, most, split=(), dtype=jnp.bfloat16):
    entries = jax.random.normal(own_key, shape, jnp.float32) * spread
    if len(split) > 0:
        entries = shard_levels(own_key, shape, split, -0.22, 0.18) * entries
    return jnp.clip(entries, min=-most, max=most).astype(dtype)


def setup_inputs(seed: int = 0) -> dict:
    streams_of = jax.random.split(jax.random.key(seed), 6)
    activations = scatter_about(streams_of[0], (TOKENS, D), 1.0, 6.0, ((0, 32), (1, 8)))
    grad_out = scatter_about(streams_of[1], (TOKENS, FF), 0.0078, 0.049804688, ((0, 32), (1, 8)))
    subspace = scatter_about(streams_of[2], (D, RANK), D ** -0.5, 0.09375)
    first_moment = scatter_about(streams_of[3], (RANK, FF), 0.3, 2.0, ((0, 32), (1, 8)), jnp.float32)
    second_moment = jnp.clip(jnp.exp(math.log(0.001) - 2.3025852 * jax.random.uniform(streams_of[4], (RANK, FF), jnp.float32) ** shard_levels(streams_of[4], (RANK, FF), ((0, 32), (1, 8)), -0.2, 0.2)), 0.0001, 0.001)
    return dict(activations=activations, grad_out=grad_out, subspace=subspace, first_moment=first_moment, second_moment=second_moment)


def reference(activations, grad_out, subspace, first_moment, second_moment):
    projected = jnp.dot(activations, subspace, preferred_element_type=jnp.float32).astype(jnp.bfloat16)
    reduced = lax.dot_general(projected, grad_out, (((0,), (0,)), ((), ())), preferred_element_type=jnp.float32)
    new_first = 0.9 * first_moment + 0.1 * reduced
    new_second = 0.999 * second_moment + 0.001 * reduced * reduced
    first_hat = new_first / (1.0 - 0.9 ** STEP)
    second_hat = new_second / (1.0 - 0.999 ** STEP)
    low_rank = (first_hat / (jnp.sqrt(second_hat) + 1e-08)).astype(jnp.bfloat16)
    update = jnp.dot(subspace, low_rank, preferred_element_type=jnp.float32).astype(jnp.bfloat16)
    return (update, new_first, new_second)
```

```python
import jax
import jax.numpy as jnp
from jax import lax
from jax.experimental import pallas as pl
from jax.experimental.pallas import tpu as pltpu
from jax.sharding import PartitionSpec as P

STEP = 10
MESH = pl.DeviceIdType.MESH
NX, NY, NZ = 4, 4, 4
KC = 4

STAGE_AT = (0.0, 5.0, 11.0, 17.0, 20.0, 24.0, 27.0, 30.0, 34.0, 36.0)
CHUNK_AFTER = 3.3


def kernel(
    a_hbm, g_hbm, s_hbm, m_hbm, v_hbm,
    up_hbm, nf_hbm, ns_hbm,
    a_v, g_v, s_v, b_v, m_v, v_v,
    xs, xo, xr, ho, zs, zr, pt, rf, cs, cr, ty, ys, yr, ws, wr, lr, acc, up_v, nf_v, ns_v,
    ld, st, xss, xrs, zss, zrs, xas, xar, css, crs, yss, yrs, wss, wrs, bss, brs, yas, yar, c2s, c2r,
):
    dp = lax.axis_index("dp")
    t = lax.axis_index("tensor")
    x, zh = t % NX, t // NX
    zl, y, c = dp // 8, (dp // 2) % NY, dp % 2
    f32, bf16 = jnp.float32, jnp.bfloat16
    rank = pt.shape[0]
    kr = rank // KC
    own = kr // (2 * NY)
    tb = a_v.shape[1]
    depth = s_v.shape[0]
    rows = b_v.shape[0]

    def x_at(d):
        return (dp, zh * NX + (x + d) % NX)

    def y_at(d):
        return (zl * 8 + ((y + d) % NY) * 2 + c, t)

    def z_at(k):
        return (k * 8 + y * 2 + c, t)

    z_far = (dp, (1 - zh) * NX + x)
    core = (dp + 1 - 2 * c, t)

    barrier = pltpu.get_barrier_semaphore()
    peers = [x_at(d) for d in range(1, NX)] + [y_at(d) for d in range(1, NY)]
    peers += [z_at((zl + d) % NZ) for d in range(1, NZ)] + [z_far, core]
    for peer in peers:
        pl.semaphore_signal(barrier, inc=1, device_id=peer, device_id_type=MESH)

    loads = [pltpu.make_async_copy(s_hbm.at[pl.ds(pl.multiple_of(t * depth, depth), depth)], s_v, ld.at[0])]
    for i, d in enumerate((1, 2, 3, 0)):
        at = pl.multiple_of(((x + d) % NX) * tb, tb)
        loads.append(pltpu.make_async_copy(a_hbm.at[pl.ds(at, tb)], a_v.at[d], ld.at[1 + i]))
    for d in range(NX):
        at = pl.multiple_of(((x + NX - d) % NX) * tb, tb)
        loads.append(pltpu.make_async_copy(g_hbm.at[pl.ds(at, tb)], g_v.at[pl.ds(d * tb, tb)], ld.at[5 + d]))
    loads.append(pltpu.make_async_copy(m_hbm, m_v, ld.at[9]))
    loads.append(pltpu.make_async_copy(v_hbm, v_v, ld.at[10]))
    loads.append(pltpu.make_async_copy(s_hbm.at[pl.ds(pl.multiple_of(dp * rows, rows), rows)], b_v, ld.at[11]))
    for load in loads:
        load.start()

    def remote(src, dst, send, recv, to):
        return pltpu.make_async_remote_copy(
            src_ref=src, dst_ref=dst, send_sem=send, recv_sem=recv, device_id=to, device_id_type=MESH
        )

    def ks(k):
        return pl.ds(k * kr, kr)

    def x_copy(k, d):
        return remote(xs.at[d - 1, ks(k)], xr.at[d - 1, ks(k)], xss.at[k, d - 1], xrs.at[k, d - 1], x_at(d))

    def z_copy(k):
        return remote(zs.at[ks(k)], zr.at[ks(k)], zss.at[k], zrs.at[k], z_far)

    def xa_copy(k, d):
        return remote(
            pt.at[ks(k), pl.ds(0, tb)], pt.at[ks(k), pl.ds(d * tb, tb)], xas.at[k, d - 1], xar.at[k, d - 1], x_at(d)
        )

    def c_copy(k):
        return remote(cs.at[k], cr.at[k], css.at[k], crs.at[k], core)

    def y_copy(k, d):
        return remote(ys.at[k, (y + d) % NY], yr.at[k, d - 1], yss.at[k, d - 1], yrs.at[k, d - 1], y_at(d))

    def w_copy(k):
        slot = (zl - k + NZ - 1) % NZ
        return remote(ws.at[k], wr.at[slot], wss.at[k], wrs.at[slot], z_at(k))

    def b_copy(k, d):
        mine = lr.at[k, y, c]
        return remote(mine, mine, bss.at[d - 1], brs.at[k], z_at((k + d) % NZ))

    def ya_copy(k, d):
        mine = lr.at[k, y, c]
        return remote(mine, mine, yas.at[k, d - 1], yar.at[k, d - 1], y_at(d))

    def ya_wait(k, d):
        theirs = lr.at[k, (y + NY - d) % NY, c]
        remote(theirs, theirs, yas.at[k, d - 1], yar.at[k, d - 1], y_at(d)).wait_recv()

    def c2_copy(k):
        half = lr.at[k, :, c]
        return remote(half, half, c2s.at[k], c2r.at[k], core)

    def c2_wait(k):
        half = lr.at[k, :, 1 - c]
        remote(half, half, c2s.at[k], c2r.at[k], core).wait_recv()

    def project(k, d):
        return lax.dot_general(
            s_v[:, k * kr : (k + 1) * kr], a_v[d], (((0,), (1,)), ((), ())), preferred_element_type=f32
        )

    def stage0(k):
        for i, d in enumerate((1, 2, 3)):
            if k == 0:
                if i == 0:
                    loads[0].wait()
                loads[1 + i].wait()
            xs[d - 1, k * kr : (k + 1) * kr] = project(k, d).astype(bf16)
            if k == 0 and i == 0:
                pl.semaphore_wait(barrier, len(peers))
            x_copy(k, d).start()
        if k == 0:
            loads[4].wait()
        xo[k * kr : (k + 1) * kr] = project(k, 0)

    def stage1(k):
        r = slice(k * kr, (k + 1) * kr)
        for d in (1, 2, 3):
            x_copy(k, d).wait_recv()
        h = xo[r] + xr[0, r].astype(f32) + xr[1, r].astype(f32) + xr[2, r].astype(f32)
        zs[r] = h.astype(bf16)
        z_copy(k).start()
        ho[r] = h

    def stage2(k):
        r = slice(k * kr, (k + 1) * kr)
        z_copy(k).wait_recv()
        pt[r, 0:tb] = (ho[r] + zr[r].astype(f32)).astype(bf16)
        for d in (1, 2, 3):
            xa_copy(k, d).start()

    def stage3(k):
        for d in (1, 2, 3):
            xa_copy(k, d).wait_recv()
        if k == 0:
            for d in range(NX):
                loads[5 + d].wait()
        red = jnp.dot(pt[k * kr : (k + 1) * kr], g_v[...], preferred_element_type=f32)
        for yy in range(NY):
            for cc in range(2):
                at = (yy * 2 + cc) * own
                rf[k, cc, yy] = red[at : at + own]
        cs[k] = rf[k, 1 - c].astype(bf16)
        c_copy(k).start()

    def stage4(k):
        c_copy(k).wait_recv()
        both = rf[k, c] + cr[k].astype(f32)
        ys[k] = both.astype(bf16)
        for d in (1, 2, 3):
            y_copy(k, d).start()
        ty[k] = both

    def stage5(k):
        for d in (1, 2, 3):
            y_copy(k, d).wait_recv()
        total = ty[k, y] + yr[k, 0].astype(f32) + yr[k, 1].astype(f32) + yr[k, 2].astype(f32)
        ty[k, y] = total

        @pl.when(zl != k)
        def _():
            ws[k] = total.astype(bf16)
            w_copy(k).start()

    def stage6(k):
        @pl.when(zl == k)
        def _():
            for d in (1, 2, 3):
                remote(ws.at[k], wr.at[d - 1], wss.at[k], wrs.at[d - 1], z_at((k + d) % NZ)).wait_recv()
            loads[9].wait()
            loads[10].wait()
            reduced = ty[k, y] + wr[0].astype(f32) + wr[1].astype(f32) + wr[2].astype(f32)
            new_first = 0.9 * m_v[...] + 0.1 * reduced
            new_second = 0.999 * v_v[...] + 0.001 * reduced * reduced
            first_hat = new_first / (1.0 - 0.9**STEP)
            second_hat = new_second / (1.0 - 0.999**STEP)
            lr[k, y, c] = (first_hat / (jnp.sqrt(second_hat) + 1e-08)).astype(bf16)
            for d in (2, 1, 3):
                b_copy(k, d).start()
            nf_v[...] = new_first
            ns_v[...] = new_second
            pltpu.make_async_copy(nf_v, nf_hbm, st.at[0]).start()
            pltpu.make_async_copy(ns_v, ns_hbm, st.at[1]).start()

    def stage7(k):
        @pl.when(zl != k)
        def _():
            b_copy(k, 1).wait_recv()

        for d in (1, 2, 3):
            ya_copy(k, d).start()

    def stage8(k):
        for d in (1, 2, 3):
            ya_wait(k, d)
        c2_copy(k).start()

    def stage9(k):
        c2_wait(k)
        if k == 0:
            loads[11].wait()
        low = lr[k].reshape(kr, lr.shape[-1])
        part = jnp.dot(b_v[:, k * kr : (k + 1) * kr], low, preferred_element_type=f32)
        if k == 0:
            acc[...] = part
        elif k < KC - 1:
            acc[...] += part
        else:
            up_v[...] = (acc[...] + part).astype(bf16)
            pltpu.make_async_copy(up_v, up_hbm, st.at[2]).start()

    stages = (stage0, stage1, stage2, stage3, stage4, stage5, stage6, stage7, stage8, stage9)
    plan = [(at + (CHUNK_AFTER * k if s else 0.1 * k), k, s) for s, at in enumerate(STAGE_AT) for k in range(KC)]
    for _, k, s in sorted(plan):
        stages[s](k)

    for k in range(KC):
        for d in (1, 2, 3):
            x_copy(k, d).wait_send()
            xa_copy(k, d).wait_send()
            y_copy(k, d).wait_send()
            ya_copy(k, d).wait_send()
        z_copy(k).wait_send()
        c_copy(k).wait_send()
        c2_copy(k).wait_send()

        @pl.when(zl != k)
        def _():
            w_copy(k).wait_send()

    for d in (1, 2, 3):
        b_copy(0, d).wait_send()
    pltpu.make_async_copy(nf_v, nf_hbm, st.at[0]).wait()
    pltpu.make_async_copy(ns_v, ns_hbm, st.at[1]).wait()
    pltpu.make_async_copy(up_v, up_hbm, st.at[2]).wait()


def local(activations, grad_out, subspace, first_moment, second_moment):
    tokens, depth = activations.shape
    ff = grad_out.shape[1]
    rank = subspace.shape[1]
    own = first_moment.shape[0]
    rows = subspace.shape[0] // lax.axis_size("dp")
    tb = tokens // NX
    kr = rank // KC
    f32, bf16 = jnp.float32, jnp.bfloat16
    dma = pltpu.SemaphoreType.DMA
    anywhere = pl.BlockSpec(memory_space=pl.ANY)
    scratch = [
        ((NX, tb, depth), bf16),
        ((tokens, ff), bf16),
        ((depth, rank), bf16),
        ((rows, rank), bf16),
        ((own, ff), f32),
        ((own, ff), f32),
        ((NX - 1, rank, tb), bf16),
        ((rank, tb), f32),
        ((NX - 1, rank, tb), bf16),
        ((rank, tb), f32),
        ((rank, tb), bf16),
        ((rank, tb), bf16),
        ((rank, tokens), bf16),
        ((KC, 2, NY, own, ff), f32),
        ((KC, NY, own, ff), bf16),
        ((KC, NY, own, ff), bf16),
        ((KC, NY, own, ff), f32),
        ((KC, NY, own, ff), bf16),
        ((KC, NY - 1, own, ff), bf16),
        ((KC, own, ff), bf16),
        ((NZ - 1, own, ff), bf16),
        ((KC, NY, 2, own, ff), bf16),
        ((rows, ff), f32),
        ((rows, ff), bf16),
        ((own, ff), f32),
        ((own, ff), f32),
    ]
    sems = [(12,), (3,), (KC, 3), (KC, 3), (KC,), (KC,), (KC, 3), (KC, 3), (KC,), (KC,), (KC, 3), (KC, 3)]
    sems += [(KC,), (3,), (3,), (KC,), (KC, 3), (KC, 3), (KC,), (KC,)]
    flops = 2 * tokens * rank * (depth + ff) + 2 * rows * rank * ff
    return pl.pallas_call(
        kernel,
        out_shape=(
            jax.ShapeDtypeStruct((rows, ff), bf16),
            jax.ShapeDtypeStruct((own, ff), f32),
            jax.ShapeDtypeStruct((own, ff), f32),
        ),
        in_specs=[anywhere] * 5,
        out_specs=(anywhere,) * 3,
        scratch_shapes=[pltpu.VMEM(shape, dtype) for shape, dtype in scratch] + [dma(shape) for shape in sems],
        compiler_params=pltpu.CompilerParams(collective_id=0, has_side_effects=True, vmem_limit_bytes=56 << 20),
        cost_estimate=pl.CostEstimate(flops=flops, bytes_accessed=8 << 20, transcendentals=own * ff),
        name="galore",
    )(activations, grad_out, subspace, first_moment, second_moment)


def solution(mesh):
    in_specs = (P("dp", "tensor"), P("dp", "tensor"), P(), P("dp", "tensor"), P("dp", "tensor"))
    out_specs = (P("dp", "tensor"), P("dp", "tensor"), P("dp", "tensor"))
    return jax.shard_map(local, mesh=mesh, in_specs=in_specs, out_specs=out_specs, check_vma=False)
```

```python
import jax
import jax.numpy as jnp
from jax import lax
from jax.experimental import pallas as pl
from jax.experimental.pallas import tpu as pltpu
from jax.sharding import PartitionSpec as P

STEP = 10
MESH = pl.DeviceIdType.MESH
NX, NY, NZ = 4, 4, 4
KC = 4

STAGE_AT = (0.0, 5.0, 11.0, 17.0, 20.0, 24.0, 27.0, 30.0, 34.0, 36.0)
CHUNK_AFTER = 2.0
TURN = (0, 3, 1, 2)


def order():
    plan = [(at + (CHUNK_AFTER * i if s else 0.1 * i), i, s) for s, at in enumerate(STAGE_AT) for i in range(KC)]
    return [(TURN[i], s) for _, i, s in sorted(plan)]


def kernel(
    a_hbm, g_hbm, s_hbm, m_hbm, v_hbm,
    up_hbm, nf_hbm, ns_hbm,
    a_v, g_v, gt, s_v, b_v, m_v, v_v,
    xs, xo, xr, ho, zs, zr, pt, rf, cs, cr, ty, ys, yr, ws, wr, lr, acc, up_v, nf_v, ns_v,
    ld, st, xss, xrs, zss, zrs, xas, xar, css, crs, yss, yrs, wss, wrs, bss, brs, yas, yar, c2s, c2r,
):
    dp = lax.axis_index("dp")
    t = lax.axis_index("tensor")
    x, zh = t % NX, t // NX
    zl, y, c = dp // 8, (dp // 2) % NY, dp % 2
    f32, bf16 = jnp.float32, jnp.bfloat16
    rank = pt.shape[0]
    kr = rank // KC
    own = kr // (2 * NY)
    tb = a_v.shape[1]
    depth = s_v.shape[0]
    rows = b_v.shape[0]

    def x_at(d):
        return (dp, zh * NX + (x + d) % NX)

    def y_at(d):
        return (zl * 8 + ((y + d) % NY) * 2 + c, t)

    def z_at(k):
        return (k * 8 + y * 2 + c, t)

    z_far = (dp, (1 - zh) * NX + x)
    core = (dp + 1 - 2 * c, t)

    barrier = pltpu.get_barrier_semaphore()
    peers = [x_at(d) for d in range(1, NX)] + [y_at(d) for d in range(1, NY)]
    peers += [z_at((zl + d) % NZ) for d in range(1, NZ)] + [z_far, core]
    for peer in peers:
        pl.semaphore_signal(barrier, inc=1, device_id=peer, device_id_type=MESH)

    loads = [pltpu.make_async_copy(s_hbm.at[pl.ds(pl.multiple_of(t * depth, depth), depth)], s_v, ld.at[0])]
    for i, d in enumerate((1, 2, 3, 0)):
        at = pl.multiple_of(((x + d) % NX) * tb, tb)
        loads.append(pltpu.make_async_copy(a_hbm.at[pl.ds(at, tb)], a_v.at[d], ld.at[1 + i]))
    for d in range(NX):
        at = pl.multiple_of(((x + NX - d) % NX) * tb, tb)
        loads.append(pltpu.make_async_copy(g_hbm.at[:, pl.ds(at, tb)], g_v.at[:, pl.ds(d * tb, tb)], ld.at[5 + d]))
    loads.append(pltpu.make_async_copy(m_hbm, m_v, ld.at[9]))
    loads.append(pltpu.make_async_copy(v_hbm, v_v, ld.at[10]))
    loads.append(pltpu.make_async_copy(s_hbm.at[pl.ds(pl.multiple_of(dp * rows, rows), rows)], b_v, ld.at[11]))
    for load in loads:
        load.start()

    def remote(src, dst, send, recv, to):
        return pltpu.make_async_remote_copy(
            src_ref=src, dst_ref=dst, send_sem=send, recv_sem=recv, device_id=to, device_id_type=MESH
        )

    def far_first(k):
        return sorted((1, 2, 3), key=lambda d: -abs((k + d) % NZ - k))

    def ks(k):
        return pl.ds(k * kr, kr)

    def x_copy(k, d):
        return remote(xs.at[d - 1, ks(k)], xr.at[d - 1, ks(k)], xss.at[k, d - 1], xrs.at[k, d - 1], x_at(d))

    def z_copy(k):
        return remote(zs.at[ks(k)], zr.at[ks(k)], zss.at[k], zrs.at[k], z_far)

    def xa_copy(k, d):
        return remote(
            pt.at[ks(k), pl.ds(0, tb)], pt.at[ks(k), pl.ds(d * tb, tb)], xas.at[k, d - 1], xar.at[k, d - 1], x_at(d)
        )

    def c_copy(k):
        return remote(cs.at[k], cr.at[k], css.at[k], crs.at[k], core)

    def y_copy(k, d):
        return remote(ys.at[k, (y + d) % NY], yr.at[k, d - 1], yss.at[k, d - 1], yrs.at[k, d - 1], y_at(d))

    def w_copy(k):
        slot = (zl - k + NZ - 1) % NZ
        return remote(ws.at[k], wr.at[slot], wss.at[k], wrs.at[slot], z_at(k))

    def b_copy(k, d):
        mine = lr.at[k, y, c]
        return remote(mine, mine, bss.at[d - 1], brs.at[k], z_at((k + d) % NZ))

    def ya_copy(k, d):
        mine = lr.at[k, y, c]
        return remote(mine, mine, yas.at[k, d - 1], yar.at[k, d - 1], y_at(d))

    def ya_wait(k, d):
        theirs = lr.at[k, (y + NY - d) % NY, c]
        remote(theirs, theirs, yas.at[k, d - 1], yar.at[k, d - 1], y_at(d)).wait_recv()

    def c2_copy(k, d):
        piece = lr.at[k, (y + NY - d) % NY, c]
        return remote(piece, piece, c2s.at[k, d], c2r.at[k, d], core)

    def c2_wait(k, d):
        piece = lr.at[k, (y + NY - d) % NY, 1 - c]
        remote(piece, piece, c2s.at[k, d], c2r.at[k, d], core).wait_recv()

    def project(k, d):
        return lax.dot_general(
            s_v[:, k * kr : (k + 1) * kr], a_v[d], (((0,), (1,)), ((), ())), preferred_element_type=f32
        )

    def stage0(k):
        for i, d in enumerate((1, 2, 3)):
            if k == TURN[0]:
                if i == 0:
                    loads[0].wait()
                loads[1 + i].wait()
            xs[d - 1, k * kr : (k + 1) * kr] = project(k, d).astype(bf16)
            if k == TURN[0] and i == 0:
                pl.semaphore_wait(barrier, len(peers))
            x_copy(k, d).start()
        if k == TURN[0]:
            loads[4].wait()
        xo[k * kr : (k + 1) * kr] = project(k, 0)

    def wait1(k):
        for d in (1, 2, 3):
            x_copy(k, d).wait_recv()

    def stage1(k):
        r = slice(k * kr, (k + 1) * kr)
        h = xo[r] + xr[0, r].astype(f32) + xr[1, r].astype(f32) + xr[2, r].astype(f32)
        zs[r] = h.astype(bf16)
        z_copy(k).start()
        ho[r] = h

    def wait2(k):
        z_copy(k).wait_recv()

    def stage2(k):
        r = slice(k * kr, (k + 1) * kr)
        pt[r, 0:tb] = (ho[r] + zr[r].astype(f32)).astype(bf16)
        for d in (1, 2, 3):
            xa_copy(k, d).start()

    def wait3(k):
        for d in (1, 2, 3):
            xa_copy(k, d).wait_recv()

    def turn_g():
        for d in range(NX):
            loads[5 + d].wait()
            gt[d * tb : (d + 1) * tb] = g_v[:, d * tb : (d + 1) * tb].T

    def stage3(k):
        red = jnp.dot(pt[k * kr : (k + 1) * kr], gt[...], preferred_element_type=f32)
        for yy in range(NY):
            for cc in range(2):
                at = (yy * 2 + cc) * own
                rf[k, cc, yy] = red[at : at + own]
        cs[k] = rf[k, 1 - c].astype(bf16)
        c_copy(k).start()

    def wait4(k):
        c_copy(k).wait_recv()

    def stage4(k):
        both = rf[k, c] + cr[k].astype(f32)
        ys[k] = both.astype(bf16)
        for d in (1, 2, 3):
            y_copy(k, d).start()
        ty[k] = both

    def wait5(k):
        for d in (1, 2, 3):
            y_copy(k, d).wait_recv()

    def stage5(k):
        total = ty[k, y] + yr[k, 0].astype(f32) + yr[k, 1].astype(f32) + yr[k, 2].astype(f32)
        ty[k, y] = total

        @pl.when(zl != k)
        def _():
            ws[k] = total.astype(bf16)
            w_copy(k).start()

    def wait6(k):
        @pl.when(zl == k)
        def _():
            for d in (1, 2, 3):
                remote(ws.at[k], wr.at[d - 1], wss.at[k], wrs.at[d - 1], z_at((k + d) % NZ)).wait_recv()

    def stage6(k):
        @pl.when(zl == k)
        def _():
            loads[9].wait()
            loads[10].wait()
            reduced = ty[k, y] + wr[0].astype(f32) + wr[1].astype(f32) + wr[2].astype(f32)
            new_first = 0.9 * m_v[...] + 0.1 * reduced
            new_second = 0.999 * v_v[...] + 0.001 * reduced * reduced
            first_hat = new_first / (1.0 - 0.9**STEP)
            second_hat = new_second / (1.0 - 0.999**STEP)
            lr[k, y, c] = (first_hat / (jnp.sqrt(second_hat) + 1e-08)).astype(bf16)
            for d in far_first(k):
                b_copy(k, d).start()
            nf_v[...] = new_first
            ns_v[...] = new_second
            pltpu.make_async_copy(nf_v, nf_hbm, st.at[0]).start()
            pltpu.make_async_copy(ns_v, ns_hbm, st.at[1]).start()

    def wait7(k):
        @pl.when(zl != k)
        def _():
            b_copy(k, 1).wait_recv()

    def stage7(k):
        for d in (2, 1, 3):
            ya_copy(k, d).start()
        c2_copy(k, 0).start()

    def wait8(k):
        for d in (1, 3, 2):
            ya_wait(k, d)
            c2_copy(k, d).start()

    def stage8(k):
        pass

    def wait9(k):
        for d in (0, 1, 3, 2):
            c2_wait(k, d)

    def stage9(k):
        if k == TURN[0]:
            loads[11].wait()
        low = lr[k].reshape(kr, lr.shape[-1])
        part = lax.dot_general(
            low, b_v[:, k * kr : (k + 1) * kr], (((0,), (1,)), ((), ())), preferred_element_type=f32
        )
        if k == TURN[0]:
            acc[...] = part
        elif k != TURN[-1]:
            acc[...] += part
        else:
            up_v[...] = (acc[...] + part).astype(bf16)
            pltpu.make_async_copy(up_v, up_hbm, st.at[2]).start()

    waits = (None, wait1, wait2, wait3, wait4, wait5, wait6, wait7, wait8, wait9)
    stages = (stage0, stage1, stage2, stage3, stage4, stage5, stage6, stage7, stage8, stage9)
    for k, s in order():
        if waits[s]:
            waits[s](k)
        stages[s](k)
        if (k, s) == (TURN[-1], 0):
            turn_g()

    for k in range(KC):
        for d in (1, 2, 3):
            x_copy(k, d).wait_send()
            xa_copy(k, d).wait_send()
            y_copy(k, d).wait_send()
            ya_copy(k, d).wait_send()
        z_copy(k).wait_send()
        c_copy(k).wait_send()
        for d in range(NY):
            c2_copy(k, d).wait_send()

        @pl.when(zl != k)
        def _():
            w_copy(k).wait_send()

    for d in (1, 2, 3):
        b_copy(0, d).wait_send()
    pltpu.make_async_copy(nf_v, nf_hbm, st.at[0]).wait()
    pltpu.make_async_copy(ns_v, ns_hbm, st.at[1]).wait()
    pltpu.make_async_copy(up_v, up_hbm, st.at[2]).wait()


def hand_on(up_in, nf_in, ns_in, up_out, nf_out, ns_out, up_v, nf_v, ns_v, sem):
    trips = ((nf_in, nf_v, nf_out), (ns_in, ns_v, ns_out), (up_in, up_v, up_out))
    reads = [pltpu.make_async_copy(src, via, sem.at[0, i]) for i, (src, via, _) in enumerate(trips)]
    writes = [pltpu.make_async_copy(via, dst, sem.at[1, i]) for i, (_, via, dst) in enumerate(trips)]
    for read in reads:
        read.start()
    for read, write in zip(reads, writes):
        read.wait()
        write.start()
    for write in writes:
        write.wait()


def local(activations, grad_out, subspace, first_moment, second_moment):
    tokens, depth = activations.shape
    ff = grad_out.shape[1]
    rank = subspace.shape[1]
    own = first_moment.shape[0]
    rows = subspace.shape[0] // lax.axis_size("dp")
    tb = tokens // NX
    kr = rank // KC
    f32, bf16 = jnp.float32, jnp.bfloat16
    dma = pltpu.SemaphoreType.DMA
    anywhere = pl.BlockSpec(memory_space=pl.ANY)
    scratch = [
        ((NX, tb, depth), bf16),
        ((ff, tokens), bf16),
        ((tokens, ff), bf16),
        ((depth, rank), bf16),
        ((rows, rank), bf16),
        ((own, ff), f32),
        ((own, ff), f32),
        ((NX - 1, rank, tb), bf16),
        ((rank, tb), f32),
        ((NX - 1, rank, tb), bf16),
        ((rank, tb), f32),
        ((rank, tb), bf16),
        ((rank, tb), bf16),
        ((rank, tokens), bf16),
        ((KC, 2, NY, own, ff), f32),
        ((KC, NY, own, ff), bf16),
        ((KC, NY, own, ff), bf16),
        ((KC, NY, own, ff), f32),
        ((KC, NY, own, ff), bf16),
        ((KC, NY - 1, own, ff), bf16),
        ((KC, own, ff), bf16),
        ((NZ - 1, own, ff), bf16),
        ((KC, NY, 2, own, ff), bf16),
        ((ff, rows), f32),
        ((ff, rows), bf16),
        ((own, ff), f32),
        ((own, ff), f32),
    ]
    sems = [(12,), (3,), (KC, 3), (KC, 3), (KC,), (KC,), (KC, 3), (KC, 3), (KC,), (KC,), (KC, 3), (KC, 3)]
    sems += [(KC,), (3,), (3,), (KC,), (KC, 3), (KC, 3), (KC, NY), (KC, NY)]
    flops = 2 * tokens * rank * (depth + ff) + 2 * rows * rank * ff
    shapes = (
        jax.ShapeDtypeStruct((ff, rows), bf16),
        jax.ShapeDtypeStruct((own, ff), f32),
        jax.ShapeDtypeStruct((own, ff), f32),
    )
    made = pl.pallas_call(
        kernel,
        out_shape=shapes,
        in_specs=[anywhere] * 5,
        out_specs=(anywhere,) * 3,
        scratch_shapes=[pltpu.VMEM(shape, dtype) for shape, dtype in scratch] + [dma(shape) for shape in sems],
        compiler_params=pltpu.CompilerParams(collective_id=0, has_side_effects=True, vmem_limit_bytes=56 << 20),
        cost_estimate=pl.CostEstimate(flops=flops, bytes_accessed=8 << 20, transcendentals=own * ff),
        name="galore",
    )(activations, grad_out.T, subspace, first_moment, second_moment)
    update, new_first, new_second = pl.pallas_call(
        hand_on,
        out_shape=shapes,
        in_specs=[anywhere] * 3,
        out_specs=(anywhere,) * 3,
        scratch_shapes=[pltpu.VMEM(made.shape, made.dtype) for made in shapes] + [dma((2, 3))],
        compiler_params=pltpu.CompilerParams(vmem_limit_bytes=56 << 20),
        name="hand_on",
    )(*made)
    return update.T, new_first, new_second


def solution(mesh):
    in_specs = (P("dp", "tensor"), P("dp", "tensor"), P(), P("dp", "tensor"), P("dp", "tensor"))
    out_specs = (P("dp", "tensor"), P("dp", "tensor"), P("dp", "tensor"))
    return jax.shard_map(local, mesh=mesh, in_specs=in_specs, out_specs=out_specs, check_vma=False)
```

```python
import jax
import jax.numpy as jnp
from jax import lax
from jax.experimental import pallas as pl
from jax.experimental.pallas import tpu as pltpu
from jax.sharding import PartitionSpec as P

STEP = 10
MESH = pl.DeviceIdType.MESH
NX, NY, NZ = 4, 4, 4
KC = 4

TURN = (0, 3, 1, 2)
CUTS = (1, 1, 1, 2)

ORDER = (
    "P10", "P11", "P12", "P20", "P13", "P21", "P22", "U00", "U10", "U01", "P23", "U11", "U02", "U20", "U12", "U21",
    "U03", "U04", "U30", "U13", "U14", "U22", "U31", "U40", "U23", "U24", "U32", "U41", "U33", "U34", "U42", "U43", "U44",
    "U50", "U52", "U51", "U60", "U53", "U54", "U62", "U61", "U63", "U64",
)


def units(ff):
    made = []
    for i, k in enumerate(TURN):
        step = -(-ff // (128 * CUTS[i])) * 128
        made += [(k, h, h * step, min(ff, (h + 1) * step)) for h in range(CUTS[i])]
    return made


def kernel(
    a_hbm, g_hbm, s_hbm, m_hbm, v_hbm,
    up_v, nf_v, ns_v,
    a_v, g_v, gt, s_v, b_v, m_v, v_v,
    xs, xo, xr, ho, zs, zr, pt, rf, cs, cr, ty, ys, yr, ws, wr, lr, acc,
    ld, xss, xrs, zss, zrs, xas, xar, css, crs, yss, yrs, wss, wrs, bss, brs, yas, yar, c2s, c2r,
):
    dp = lax.axis_index("dp")
    t = lax.axis_index("tensor")
    x, zh = t % NX, t // NX
    zl, y, c = dp // 8, (dp // 2) % NY, dp % 2
    f32, bf16 = jnp.float32, jnp.bfloat16
    rank = s_v.shape[1]
    ff = gt.shape[1]
    kr = rank // KC
    own = kr // (2 * NY)
    tb = a_v.shape[1]
    depth = s_v.shape[0]
    rows = b_v.shape[0]
    unit = units(ff)

    def x_at(d):
        return (dp, zh * NX + (x + d) % NX)

    def y_at(d):
        return (zl * 8 + ((y + d) % NY) * 2 + c, t)

    def z_at(k):
        return (k * 8 + y * 2 + c, t)

    z_far = (dp, (1 - zh) * NX + x)
    core = (dp + 1 - 2 * c, t)

    barrier = pltpu.get_barrier_semaphore()
    peers = [x_at(d) for d in range(1, NX)] + [y_at(d) for d in range(1, NY)]
    peers += [z_at((zl + d) % NZ) for d in range(1, NZ)] + [z_far, core]
    loads = [pltpu.make_async_copy(s_hbm.at[pl.ds(pl.multiple_of(t * depth, depth), depth)], s_v, ld.at[0])]
    for i, d in enumerate((1, 2, 3, 0)):
        at = pl.multiple_of(((x + d) % NX) * tb, tb)
        loads.append(pltpu.make_async_copy(a_hbm.at[pl.ds(at, tb)], a_v.at[d], ld.at[1 + i]))
    for d in range(NX):
        at = pl.multiple_of(((x + NX - d) % NX) * tb, tb)
        loads.append(pltpu.make_async_copy(g_hbm.at[:, pl.ds(at, tb)], g_v.at[:, pl.ds(d * tb, tb)], ld.at[5 + d]))
    loads.append(pltpu.make_async_copy(m_hbm, m_v, ld.at[9]))
    loads.append(pltpu.make_async_copy(v_hbm, v_v, ld.at[10]))
    loads.append(pltpu.make_async_copy(s_hbm.at[pl.ds(pl.multiple_of(dp * rows, rows), rows)], b_v, ld.at[11]))
    for load in loads[:5]:
        load.start()
    for peer in peers:
        pl.semaphore_signal(barrier, inc=1, device_id=peer, device_id_type=MESH)

    def remote(src, dst, send, recv, to):
        return pltpu.make_async_remote_copy(
            src_ref=src, dst_ref=dst, send_sem=send, recv_sem=recv, device_id=to, device_id_type=MESH
        )

    def span(k):
        return slice(k * kr, (k + 1) * kr)

    def rows_of(k):
        return pl.ds(k * kr, kr)

    def slot(d):
        return pl.ds(d * tb, tb)

    def x_copy(k, d):
        r = rows_of(k)
        return remote(xs.at[d - 1, r], xr.at[d - 1, r], xss.at[k, d - 1], xrs.at[k, d - 1], x_at(d))

    def z_copy(k):
        r = rows_of(k)
        return remote(zs.at[r], zr.at[r], zss.at[k], zrs.at[k], z_far)

    def xa_copy(k, d):
        src, dst = pt.at[k, :, :, :, slot(0)], pt.at[k, :, :, :, slot(d)]
        return remote(src, dst, xas.at[k, d - 1], xar.at[k, d - 1], x_at(d))

    def project(k, d):
        return lax.dot_general(s_v[:, span(k)], a_v[d], (((0,), (1,)), ((), ())), preferred_element_type=f32)

    def send_partial(k):
        first = k == TURN[0]
        if first:
            loads[0].wait()
        for d in (2, 1, 3):
            if first:
                loads[d].wait()
            xs[d - 1, span(k)] = project(k, d).astype(bf16)
            if first and d == 2:
                pl.semaphore_wait(barrier, len(peers))
            x_copy(k, d).start()
        if first:
            for load in loads[5:]:
                load.start()
            loads[4].wait()
        xo[span(k)] = project(k, 0)

    def turn_g():
        for d in range(NX):
            loads[5 + d].wait()
            gt[d * tb : (d + 1) * tb] = g_v[:, d * tb : (d + 1) * tb].T

    def piece1(i):
        k = TURN[i]
        r = span(k)
        for d in (1, 3, 2):
            x_copy(k, d).wait_recv()
        h = xo[r] + xr[0, r].astype(f32) + xr[1, r].astype(f32) + xr[2, r].astype(f32)
        zs[r] = h.astype(bf16)
        z_copy(k).start()
        ho[r] = h

    def piece2(i):
        k = TURN[i]
        r = span(k)
        z_copy(k).wait_recv()
        pt[k, :, :, :, 0:tb] = (ho[r] + zr[r].astype(f32)).astype(bf16).reshape(NY, 2, own, tb)
        for d in (2, 1, 3):
            xa_copy(k, d).start()

    def cols(u):
        return pl.ds(unit[u][2], unit[u][3] - unit[u][2])

    def c_copy(u):
        k = unit[u][0]
        return remote(cs.at[k, :, :, cols(u)], cr.at[k, :, :, cols(u)], css.at[u], crs.at[u], core)

    def y_copy(u, d):
        k = unit[u][0]
        src, dst = ys.at[k, (y + d) % NY, :, cols(u)], yr.at[k, d - 1, :, cols(u)]
        return remote(src, dst, yss.at[u, d - 1], yrs.at[u, d - 1], y_at(d))

    def w_copy(u):
        k, h = unit[u][:2]
        place = (zl - k + NZ - 1) % NZ
        return remote(ws.at[k, :, cols(u)], wr.at[place, :, cols(u)], wss.at[u], wrs.at[h, place], z_at(k))

    def w_wait(u, d):
        k, h = unit[u][:2]
        theirs = wr.at[d - 1, :, cols(u)]
        remote(theirs, theirs, wss.at[u], wrs.at[h, d - 1], z_at((k + d) % NZ)).wait_recv()

    def b_copy(u, d):
        k, h = unit[u][:2]
        mine = lr.at[k, y, c, :, cols(u)]
        return remote(mine, mine, bss.at[h, d - 1], brs.at[u], z_at((k + d) % NZ))

    def ya_copy(u, d):
        mine = lr.at[unit[u][0], y, c, :, cols(u)]
        return remote(mine, mine, yas.at[u, d - 1], yar.at[u, d - 1], y_at(d))

    def ya_wait(u, d):
        theirs = lr.at[unit[u][0], (y + NY - d) % NY, c, :, cols(u)]
        remote(theirs, theirs, yas.at[u, d - 1], yar.at[u, d - 1], y_at(d)).wait_recv()

    def c2_copy(u, d):
        mine = lr.at[unit[u][0], (y + NY - d) % NY, c, :, cols(u)]
        return remote(mine, mine, c2s.at[u, d], c2r.at[u, d], core)

    def c2_wait(u, d):
        theirs = lr.at[unit[u][0], (y + NY - d) % NY, 1 - c, :, cols(u)]
        remote(theirs, theirs, c2s.at[u, d], c2r.at[u, d], core).wait_recv()

    def unit0(u):
        k, h, lo, hi = unit[u]
        if h == 0:
            for d in (1, 3, 2):
                xa_copy(k, d).wait_recv()

        def product(parity):
            p = pt[k, :, parity].reshape(NY * own, pt.shape[-1])
            return jnp.dot(p, gt[:, lo:hi], preferred_element_type=f32).reshape(NY, own, hi - lo)

        cs[k, :, :, lo:hi] = product(1 - c).astype(bf16)
        c_copy(u).start()
        rf[k, :, :, lo:hi] = product(c)

    def unit1(u):
        k, h, lo, hi = unit[u]
        c_copy(u).wait_recv()
        both = rf[k, :, :, lo:hi] + cr[k, :, :, lo:hi].astype(f32)
        ys[k, :, :, lo:hi] = both.astype(bf16)
        for d in (2, 1, 3):
            y_copy(u, d).start()
        ty[k, :, :, lo:hi] = both

    def unit2(u):
        k, h, lo, hi = unit[u]
        for d in (1, 3, 2):
            y_copy(u, d).wait_recv()
        total = ty[k, y, :, lo:hi]
        for d in (1, 2, 3):
            total = total + yr[k, d - 1, :, lo:hi].astype(f32)
        ty[k, y, :, lo:hi] = total

        @pl.when(zl != k)
        def _():
            ws[k, :, lo:hi] = total.astype(bf16)
            w_copy(u).start()

    def far_first(k):
        return sorted((1, 2, 3), key=lambda d: -abs((k + d) % NZ - k))

    def unit3(u):
        k, h, lo, hi = unit[u]

        @pl.when(zl == k)
        def _():
            for d in (1, 2, 3):
                w_wait(u, d)
            if h == 0:
                loads[9].wait()
                loads[10].wait()
            reduced = ty[k, y, :, lo:hi]
            for d in (1, 2, 3):
                reduced = reduced + wr[d - 1, :, lo:hi].astype(f32)
            first, second = m_v[:, lo:hi], v_v[:, lo:hi]
            first_hat = (0.9 / (1.0 - 0.9**STEP)) * first + (0.1 / (1.0 - 0.9**STEP)) * reduced
            second_hat = (0.999 / (1.0 - 0.999**STEP)) * second + (0.001 / (1.0 - 0.999**STEP)) * reduced * reduced
            lr[k, y, c, :, lo:hi] = (first_hat / (jnp.sqrt(second_hat) + 1e-08)).astype(bf16)
            for d in far_first(k):
                b_copy(u, d).start()
            nf_v[:, lo:hi] = 0.9 * first + 0.1 * reduced
            ns_v[:, lo:hi] = 0.999 * second + 0.001 * reduced * reduced

    def unit4(u):
        @pl.when(zl != unit[u][0])
        def _():
            b_copy(u, 1).wait_recv()

        for d in (2, 1, 3):
            ya_copy(u, d).start()
        c2_copy(u, 0).start()

    def unit5(u):
        for d in (1, 3, 2):
            ya_wait(u, d)
            c2_copy(u, d).start()

    def unit6(u):
        k, h, lo, hi = unit[u]
        for d in (0, 1, 3, 2):
            c2_wait(u, d)
        if u == 0:
            loads[11].wait()
        low = lr[k, :, :, :, lo:hi].reshape(kr, hi - lo)
        part = lax.dot_general(
            low, b_v[:, k * kr : (k + 1) * kr], (((0,), (1,)), ((), ())), preferred_element_type=f32
        )
        if k == TURN[0]:
            acc[lo:hi] = part
        elif k != TURN[-1]:
            acc[lo:hi] += part
        else:
            up_v[lo:hi] = (acc[lo:hi] + part).astype(bf16)

    for k in TURN:
        send_partial(k)
    turn_g()
    stages = dict(P=(None, piece1, piece2), U=(unit0, unit1, unit2, unit3, unit4, unit5, unit6))
    for name in ORDER:
        stages[name[0]][int(name[1])](int(name[2]))

    for k in TURN:
        for d in (1, 2, 3):
            x_copy(k, d).wait_send()
            xa_copy(k, d).wait_send()
        z_copy(k).wait_send()
    for u, (k, h, _, _) in enumerate(unit):
        c_copy(u).wait_send()
        for d in (1, 2, 3):
            y_copy(u, d).wait_send()
            ya_copy(u, d).wait_send()
        for d in range(NY):
            c2_copy(u, d).wait_send()

        @pl.when(zl != k)
        def _():
            w_copy(u).wait_send()

        @pl.when(zl == k)
        def _():
            for d in (1, 2, 3):
                b_copy(u, d).wait_send()


def hand_on(up_in, nf_in, ns_in, up_out, nf_out, ns_out, sem):
    pairs = ((up_in, up_out), (nf_in, nf_out), (ns_in, ns_out))
    writes = [pltpu.make_async_copy(src, dst, sem.at[i]) for i, (src, dst) in enumerate(pairs)]
    for write in writes:
        write.start()
    for write in writes:
        write.wait()


def local(activations, grad_out, subspace, first_moment, second_moment):
    tokens, depth = activations.shape
    ff = grad_out.shape[1]
    rank = subspace.shape[1]
    own = first_moment.shape[0]
    rows = subspace.shape[0] // lax.axis_size("dp")
    tb = tokens // NX
    kr = rank // KC
    f32, bf16 = jnp.float32, jnp.bfloat16
    dma = pltpu.SemaphoreType.DMA
    anywhere = pl.BlockSpec(memory_space=pl.ANY)
    scratch = [
        ((NX, tb, depth), bf16),
        ((ff, tokens), bf16),
        ((tokens, ff), bf16),
        ((depth, rank), bf16),
        ((rows, rank), bf16),
        ((own, ff), f32),
        ((own, ff), f32),
        ((NX - 1, rank, tb), bf16),
        ((rank, tb), f32),
        ((NX - 1, rank, tb), bf16),
        ((rank, tb), f32),
        ((rank, tb), bf16),
        ((rank, tb), bf16),
        ((KC, NY, 2, own, tokens), bf16),
        ((KC, NY, own, ff), f32),
        ((KC, NY, own, ff), bf16),
        ((KC, NY, own, ff), bf16),
        ((KC, NY, own, ff), f32),
        ((KC, NY, own, ff), bf16),
        ((KC, NY - 1, own, ff), bf16),
        ((KC, own, ff), bf16),
        ((NZ - 1, own, ff), bf16),
        ((KC, NY, 2, own, ff), bf16),
        ((ff, rows), f32),
    ]
    nu, nh = len(units(ff)), max(CUTS)
    sems = [(12,), (KC, 3), (KC, 3), (KC,), (KC,), (KC, 3), (KC, 3)]
    sems += [(nu,), (nu,), (nu, 3), (nu, 3), (nu,), (nh, 3), (nh, 3), (nu,), (nu, 3), (nu, 3), (nu, NY), (nu, NY)]
    flops = 2 * tokens * rank * (depth + ff) + 2 * rows * rank * ff
    shapes = (
        jax.ShapeDtypeStruct((ff, rows), bf16),
        jax.ShapeDtypeStruct((own, ff), f32),
        jax.ShapeDtypeStruct((own, ff), f32),
    )
    made = pl.pallas_call(
        kernel,
        out_shape=tuple(pltpu.VMEM(out.shape, out.dtype) for out in shapes),
        in_specs=[anywhere] * 5,
        out_specs=(pl.BlockSpec(memory_space=pltpu.VMEM),) * 3,
        scratch_shapes=[pltpu.VMEM(shape, dtype) for shape, dtype in scratch] + [dma(shape) for shape in sems],
        compiler_params=pltpu.CompilerParams(collective_id=0, has_side_effects=True, vmem_limit_bytes=56 << 20),
        cost_estimate=pl.CostEstimate(flops=flops, bytes_accessed=8 << 20, transcendentals=own * ff),
        name="galore",
    )(activations, grad_out.T, subspace, first_moment, second_moment)
    update, new_first, new_second = pl.pallas_call(
        hand_on,
        out_shape=shapes,
        in_specs=[anywhere] * 3,
        out_specs=(anywhere,) * 3,
        scratch_shapes=[dma((3,))],
        name="hand_on",
    )(*[pltpu.with_memory_space_constraint(one, pltpu.VMEM) for one in made])
    return update.T, new_first, new_second


def solution(mesh):
    in_specs = (P("dp", "tensor"), P("dp", "tensor"), P(), P("dp", "tensor"), P("dp", "tensor"))
    out_specs = (P("dp", "tensor"), P("dp", "tensor"), P("dp", "tensor"))
    return jax.shard_map(local, mesh=mesh, in_specs=in_specs, out_specs=out_specs, check_vma=False)
```

```python
import jax
import jax.numpy as jnp
from jax import lax
from jax.experimental import pallas as pl
from jax.experimental.pallas import tpu as pltpu
from jax.sharding import PartitionSpec as P

STEP = 10
MESH = pl.DeviceIdType.MESH
NX, NY, NZ = 4, 4, 4
KC = 4

TURN = (3, 1, 2, 0)
CUTS = (1, 1, 1, 2)

ORDER = (
    "P10", "P11", "P12", "P20", "P13", "P21", "P22", "U00", "U10", "U01", "P23", "U11", "U02", "U20", "U12", "U21",
    "U03", "U04", "U30", "U13", "U14", "U22", "U31", "U40", "U23", "U24", "U32", "U41", "U33", "U34", "U42", "U43", "U44",
    "U50", "U52", "U51", "U60", "U53", "U54", "U62", "U61", "U63", "U64",
)


def units(ff):
    made = []
    for i, k in enumerate(TURN):
        step = -(-ff // (128 * CUTS[i])) * 128
        made += [(k, h, h * step, min(ff, (h + 1) * step)) for h in range(CUTS[i])]
    return made


def kernel(
    a_hbm, g_hbm, s_hbm, m_hbm, v_hbm,
    up_v, nf_v, ns_v,
    a_v, g_v, gt, s_v, b_v, m_v, v_v,
    xs, xo, xr, ho, zs, zr, pt, rf, cs, cr, ty, ys, yr, ws, wr, lr, acc,
    ld, xss, xrs, zss, zrs, xas, xar, css, crs, yss, yrs, wss, wrs, bss, brs, yas, yar, c2s, c2r,
):
    dp = lax.axis_index("dp")
    t = lax.axis_index("tensor")
    x, zh = t % NX, t // NX
    zl, y, c = dp // 8, (dp // 2) % NY, dp % 2
    f32, bf16 = jnp.float32, jnp.bfloat16
    rank = s_v.shape[1]
    ff = gt.shape[1]
    kr = rank // KC
    own = kr // (2 * NY)
    tb = a_v.shape[1]
    depth = s_v.shape[0]
    rows = b_v.shape[0]
    unit = units(ff)

    def x_at(d):
        return (dp, zh * NX + (x + d) % NX)

    def y_at(d):
        return (zl * 8 + ((y + d) % NY) * 2 + c, t)

    def z_at(k):
        return (k * 8 + y * 2 + c, t)

    z_far = (dp, (1 - zh) * NX + x)
    core = (dp + 1 - 2 * c, t)

    barrier = pltpu.get_barrier_semaphore()
    peers = [x_at(d) for d in range(1, NX)] + [y_at(d) for d in range(1, NY)]
    peers += [z_at((zl + d) % NZ) for d in range(1, NZ)] + [z_far, core]
    loads = [pltpu.make_async_copy(s_hbm.at[pl.ds(pl.multiple_of(t * depth, depth), depth)], s_v, ld.at[0])]
    for i, d in enumerate((1, 2, 3, 0)):
        at = pl.multiple_of(((x + d) % NX) * tb, tb)
        loads.append(pltpu.make_async_copy(a_hbm.at[pl.ds(at, tb)], a_v.at[d], ld.at[1 + i]))
    for d in range(NX):
        at = pl.multiple_of(((x + NX - d) % NX) * tb, tb)
        loads.append(pltpu.make_async_copy(g_hbm.at[:, pl.ds(at, tb)], g_v.at[:, pl.ds(d * tb, tb)], ld.at[5 + d]))
    loads.append(pltpu.make_async_copy(m_hbm, m_v, ld.at[9]))
    loads.append(pltpu.make_async_copy(v_hbm, v_v, ld.at[10]))
    loads.append(pltpu.make_async_copy(s_hbm.at[pl.ds(pl.multiple_of(dp * rows, rows), rows)], b_v, ld.at[11]))
    for load in loads[:5]:
        load.start()
    for peer in peers:
        pl.semaphore_signal(barrier, inc=1, device_id=peer, device_id_type=MESH)

    def remote(src, dst, send, recv, to):
        return pltpu.make_async_remote_copy(
            src_ref=src, dst_ref=dst, send_sem=send, recv_sem=recv, device_id=to, device_id_type=MESH
        )

    def span(k):
        return slice(k * kr, (k + 1) * kr)

    def rows_of(k):
        return pl.ds(k * kr, kr)

    def slot(d):
        return pl.ds(d * tb, tb)

    def x_copy(k, d):
        r = rows_of(k)
        return remote(xs.at[d - 1, r], xr.at[d - 1, r], xss.at[k, d - 1], xrs.at[k, d - 1], x_at(d))

    def z_copy(k):
        r = rows_of(k)
        return remote(zs.at[r], zr.at[r], zss.at[k], zrs.at[k], z_far)

    def xa_copy(k, d):
        src, dst = pt.at[k, :, :, :, slot(0)], pt.at[k, :, :, :, slot(d)]
        return remote(src, dst, xas.at[k, d - 1], xar.at[k, d - 1], x_at(d))

    def project(k, d):
        return lax.dot_general(s_v[:, span(k)], a_v[d], (((0,), (1,)), ((), ())), preferred_element_type=f32)

    def send_partial(k):
        first = k == TURN[0]
        if first:
            loads[0].wait()
        for d in (2, 1, 3):
            if first:
                loads[d].wait()
            xs[d - 1, span(k)] = project(k, d).astype(bf16)
            if first and d == 2:
                pl.semaphore_wait(barrier, len(peers))
            x_copy(k, d).start()
        if first:
            for load in loads[5:]:
                load.start()
            loads[4].wait()
        xo[span(k)] = project(k, 0)

    def turn_g():
        for d in range(NX):
            loads[5 + d].wait()
            gt[d * tb : (d + 1) * tb] = g_v[:, d * tb : (d + 1) * tb].T

    def piece1(i):
        k = TURN[i]
        r = span(k)
        for d in (1, 3, 2):
            x_copy(k, d).wait_recv()
        h = xo[r] + xr[0, r].astype(f32) + xr[1, r].astype(f32) + xr[2, r].astype(f32)
        zs[r] = h.astype(bf16)
        z_copy(k).start()
        ho[r] = h

    def piece2(i):
        k = TURN[i]
        r = span(k)
        z_copy(k).wait_recv()
        pt[k, :, :, :, 0:tb] = (ho[r] + zr[r].astype(f32)).astype(bf16).reshape(NY, 2, own, tb)
        for d in (2, 1, 3):
            xa_copy(k, d).start()

    def cols(u):
        return pl.ds(unit[u][2], unit[u][3] - unit[u][2])

    def c_copy(u):
        k = unit[u][0]
        return remote(cs.at[k, :, :, cols(u)], cr.at[k, :, :, cols(u)], css.at[u], crs.at[u], core)

    def y_copy(u, d):
        k = unit[u][0]
        src, dst = ys.at[k, (y + d) % NY, :, cols(u)], yr.at[k, d - 1, :, cols(u)]
        return remote(src, dst, yss.at[u, d - 1], yrs.at[u, d - 1], y_at(d))

    def w_copy(u):
        k, h = unit[u][:2]
        place = (zl - k + NZ - 1) % NZ
        return remote(ws.at[k, :, cols(u)], wr.at[place, :, cols(u)], wss.at[u], wrs.at[h, place], z_at(k))

    def w_wait(u, d):
        k, h = unit[u][:2]
        theirs = wr.at[d - 1, :, cols(u)]
        remote(theirs, theirs, wss.at[u], wrs.at[h, d - 1], z_at((k + d) % NZ)).wait_recv()

    def b_copy(u, d):
        k, h = unit[u][:2]
        mine = lr.at[k, y, c, :, cols(u)]
        return remote(mine, mine, bss.at[h, d - 1], brs.at[u], z_at((k + d) % NZ))

    def ya_copy(u, d):
        mine = lr.at[unit[u][0], y, c, :, cols(u)]
        return remote(mine, mine, yas.at[u, d - 1], yar.at[u, d - 1], y_at(d))

    def ya_wait(u, d):
        theirs = lr.at[unit[u][0], (y + NY - d) % NY, c, :, cols(u)]
        remote(theirs, theirs, yas.at[u, d - 1], yar.at[u, d - 1], y_at(d)).wait_recv()

    def c2_copy(u, d):
        mine = lr.at[unit[u][0], (y + NY - d) % NY, c, :, cols(u)]
        return remote(mine, mine, c2s.at[u, d], c2r.at[u, d], core)

    def c2_wait(u, d):
        theirs = lr.at[unit[u][0], (y + NY - d) % NY, 1 - c, :, cols(u)]
        remote(theirs, theirs, c2s.at[u, d], c2r.at[u, d], core).wait_recv()

    def unit0(u):
        k, h, lo, hi = unit[u]
        if h == 0:
            for d in (1, 3, 2):
                xa_copy(k, d).wait_recv()

        def product(parity):
            p = pt[k, :, parity].reshape(NY * own, pt.shape[-1])
            return jnp.dot(p, gt[:, lo:hi], preferred_element_type=f32).reshape(NY, own, hi - lo)

        cs[k, :, :, lo:hi] = product(1 - c).astype(bf16)
        c_copy(u).start()
        rf[k, :, :, lo:hi] = product(c)

    def unit1(u):
        k, h, lo, hi = unit[u]
        c_copy(u).wait_recv()
        both = rf[k, :, :, lo:hi] + cr[k, :, :, lo:hi].astype(f32)
        ys[k, :, :, lo:hi] = both.astype(bf16)
        for d in (2, 1, 3):
            y_copy(u, d).start()
        ty[k, :, :, lo:hi] = both

    def unit2(u):
        k, h, lo, hi = unit[u]
        for d in (1, 3, 2):
            y_copy(u, d).wait_recv()
        total = ty[k, y, :, lo:hi]
        for d in (1, 2, 3):
            total = total + yr[k, d - 1, :, lo:hi].astype(f32)
        ty[k, y, :, lo:hi] = total

        @pl.when(zl != k)
        def _():
            ws[k, :, lo:hi] = total.astype(bf16)
            w_copy(u).start()

    def far_first(k):
        return sorted((1, 2, 3), key=lambda d: -abs((k + d) % NZ - k))

    def unit3(u):
        k, h, lo, hi = unit[u]

        @pl.when(zl == k)
        def _():
            for d in (1, 2, 3):
                w_wait(u, d)
            if h == 0:
                loads[9].wait()
                loads[10].wait()
            reduced = ty[k, y, :, lo:hi]
            for d in (1, 2, 3):
                reduced = reduced + wr[d - 1, :, lo:hi].astype(f32)
            first, second = m_v[:, lo:hi], v_v[:, lo:hi]
            first_hat = (0.9 / (1.0 - 0.9**STEP)) * first + (0.1 / (1.0 - 0.9**STEP)) * reduced
            second_hat = (0.999 / (1.0 - 0.999**STEP)) * second + (0.001 / (1.0 - 0.999**STEP)) * reduced * reduced
            lr[k, y, c, :, lo:hi] = (first_hat / (jnp.sqrt(second_hat) + 1e-08)).astype(bf16)
            for d in far_first(k):
                b_copy(u, d).start()
            nf_v[:, lo:hi] = 0.9 * first + 0.1 * reduced
            ns_v[:, lo:hi] = 0.999 * second + 0.001 * reduced * reduced

    def unit4(u):
        @pl.when(zl != unit[u][0])
        def _():
            b_copy(u, 1).wait_recv()

        for d in (2, 1, 3):
            ya_copy(u, d).start()
        c2_copy(u, 0).start()

    def unit5(u):
        for d in (1, 3, 2):
            ya_wait(u, d)
            c2_copy(u, d).start()

    def unit6(u):
        k, h, lo, hi = unit[u]
        for d in (0, 1, 3, 2):
            c2_wait(u, d)
        if u == 0:
            loads[11].wait()
        low = lr[k, :, :, :, lo:hi].reshape(kr, hi - lo)
        part = lax.dot_general(
            low, b_v[:, k * kr : (k + 1) * kr], (((0,), (1,)), ((), ())), preferred_element_type=f32
        )
        if k == TURN[0]:
            acc[lo:hi] = part
        elif k != TURN[-1]:
            acc[lo:hi] += part
        else:
            up_v[lo:hi] = (acc[lo:hi] + part).astype(bf16)

    for k in TURN:
        send_partial(k)
    turn_g()
    stages = dict(P=(None, piece1, piece2), U=(unit0, unit1, unit2, unit3, unit4, unit5, unit6))
    for name in ORDER:
        stages[name[0]][int(name[1])](int(name[2]))

    for k in TURN:
        for d in (1, 2, 3):
            x_copy(k, d).wait_send()
            xa_copy(k, d).wait_send()
        z_copy(k).wait_send()
    for u, (k, h, _, _) in enumerate(unit):
        c_copy(u).wait_send()
        for d in (1, 2, 3):
            y_copy(u, d).wait_send()
            ya_copy(u, d).wait_send()
        for d in range(NY):
            c2_copy(u, d).wait_send()

        @pl.when(zl != k)
        def _():
            w_copy(u).wait_send()

        @pl.when(zl == k)
        def _():
            for d in (1, 2, 3):
                b_copy(u, d).wait_send()


def hand_on(up_in, nf_in, ns_in, up_out, nf_out, ns_out, sem):
    pairs = ((up_in, up_out), (nf_in, nf_out), (ns_in, ns_out))
    writes = [pltpu.make_async_copy(src, dst, sem.at[i]) for i, (src, dst) in enumerate(pairs)]
    for write in writes:
        write.start()
    for write in writes:
        write.wait()


def local(activations, grad_out, subspace, first_moment, second_moment):
    tokens, depth = activations.shape
    ff = grad_out.shape[1]
    rank = subspace.shape[1]
    own = first_moment.shape[0]
    rows = subspace.shape[0] // lax.axis_size("dp")
    tb = tokens // NX
    kr = rank // KC
    f32, bf16 = jnp.float32, jnp.bfloat16
    dma = pltpu.SemaphoreType.DMA
    anywhere = pl.BlockSpec(memory_space=pl.ANY)
    scratch = [
        ((NX, tb, depth), bf16),
        ((ff, tokens), bf16),
        ((tokens, ff), bf16),
        ((depth, rank), bf16),
        ((rows, rank), bf16),
        ((own, ff), f32),
        ((own, ff), f32),
        ((NX - 1, rank, tb), bf16),
        ((rank, tb), f32),
        ((NX - 1, rank, tb), bf16),
        ((rank, tb), f32),
        ((rank, tb), bf16),
        ((rank, tb), bf16),
        ((KC, NY, 2, own, tokens), bf16),
        ((KC, NY, own, ff), f32),
        ((KC, NY, own, ff), bf16),
        ((KC, NY, own, ff), bf16),
        ((KC, NY, own, ff), f32),
        ((KC, NY, own, ff), bf16),
        ((KC, NY - 1, own, ff), bf16),
        ((KC, own, ff), bf16),
        ((NZ - 1, own, ff), bf16),
        ((KC, NY, 2, own, ff), bf16),
        ((ff, rows), f32),
    ]
    nu, nh = len(units(ff)), max(CUTS)
    sems = [(12,), (KC, 3), (KC, 3), (KC,), (KC,), (KC, 3), (KC, 3)]
    sems += [(nu,), (nu,), (nu, 3), (nu, 3), (nu,), (nh, 3), (nh, 3), (nu,), (nu, 3), (nu, 3), (nu, NY), (nu, NY)]
    flops = 2 * tokens * rank * (depth + ff) + 2 * rows * rank * ff
    shapes = (
        jax.ShapeDtypeStruct((ff, rows), bf16),
        jax.ShapeDtypeStruct((own, ff), f32),
        jax.ShapeDtypeStruct((own, ff), f32),
    )
    made = pl.pallas_call(
        kernel,
        out_shape=tuple(pltpu.VMEM(out.shape, out.dtype) for out in shapes),
        in_specs=[anywhere] * 5,
        out_specs=(pl.BlockSpec(memory_space=pltpu.VMEM),) * 3,
        scratch_shapes=[pltpu.VMEM(shape, dtype) for shape, dtype in scratch] + [dma(shape) for shape in sems],
        compiler_params=pltpu.CompilerParams(collective_id=0, has_side_effects=True, vmem_limit_bytes=56 << 20),
        cost_estimate=pl.CostEstimate(flops=flops, bytes_accessed=8 << 20, transcendentals=own * ff),
        name="galore",
    )(activations, grad_out.T, subspace, first_moment, second_moment)
    update, new_first, new_second = pl.pallas_call(
        hand_on,
        out_shape=shapes,
        in_specs=[anywhere] * 3,
        out_specs=(anywhere,) * 3,
        scratch_shapes=[dma((3,))],
        name="hand_on",
    )(*[pltpu.with_memory_space_constraint(one, pltpu.VMEM) for one in made])
    return update.T, new_first, new_second


def solution(mesh):
    in_specs = (P("dp", "tensor"), P("dp", "tensor"), P(), P("dp", "tensor"), P("dp", "tensor"))
    out_specs = (P("dp", "tensor"), P("dp", "tensor"), P("dp", "tensor"))
    return jax.shard_map(local, mesh=mesh, in_specs=in_specs, out_specs=out_specs, check_vma=False)
```

```python
import jax
import jax.numpy as jnp
from jax import lax
from jax.experimental import pallas as pl
from jax.experimental.pallas import tpu as pltpu
from jax.sharding import PartitionSpec as P

STEP = 10
MESH = pl.DeviceIdType.MESH
NX, NY, NZ = 4, 4, 4
KC = 4

TURN = (3, 1, 2, 0)
CUTS = (1, 1, 1, 2)

ORDER = (
    "P10", "P11", "P12", "P20", "P13", "P21", "P22", "U00", "U10", "U01", "P23", "U11", "U02", "U20", "U12", "U21",
    "U03", "U04", "U30", "U13", "U14", "U22", "U31", "U40", "U23", "U24", "U32", "U41", "U33", "U34", "U50", "U42", "U51",
    "U43", "U44", "U60", "U61", "U52", "U53", "U54", "U62", "U63", "U64",
)


def units(ff):
    made = []
    for i, k in enumerate(TURN):
        step = -(-ff // (128 * CUTS[i])) * 128
        made += [(k, h, h * step, min(ff, (h + 1) * step)) for h in range(CUTS[i])]
    return made


def kernel(
    a_hbm, g_hbm, s_hbm, m_hbm, v_hbm,
    up_v, nf_v, ns_v,
    a_v, g_v, gt, s_v, b_v, m_v, v_v,
    xs, xo, xr, ho, zs, zr, pt, rf, cs, cr, ty, ys, yr, ws, wr, lr, acc,
    ld, xss, xrs, zss, zrs, xas, xar, css, crs, yss, yrs, wss, wrs, bss, brs, yas, yar, c2s, c2r,
):
    dp = lax.axis_index("dp")
    t = lax.axis_index("tensor")
    x, zh = t % NX, t // NX
    zl, y, c = dp // 8, (dp // 2) % NY, dp % 2
    f32, bf16 = jnp.float32, jnp.bfloat16
    rank = s_v.shape[1]
    ff = gt.shape[1]
    kr = rank // KC
    own = kr // (2 * NY)
    tb = a_v.shape[1]
    depth = s_v.shape[0]
    rows = b_v.shape[0]
    unit = units(ff)

    def x_at(d):
        return (dp, zh * NX + (x + d) % NX)

    def y_at(d):
        return (zl * 8 + ((y + d) % NY) * 2 + c, t)

    def z_at(k):
        return (k * 8 + y * 2 + c, t)

    z_far = (dp, (1 - zh) * NX + x)
    core = (dp + 1 - 2 * c, t)

    barrier = pltpu.get_barrier_semaphore()
    peers = [x_at(d) for d in range(1, NX)] + [y_at(d) for d in range(1, NY)]
    peers += [z_at((zl + d) % NZ) for d in range(1, NZ)] + [z_far, core]
    loads = [pltpu.make_async_copy(s_hbm.at[pl.ds(pl.multiple_of(t * depth, depth), depth)], s_v, ld.at[0])]
    for i, d in enumerate((1, 2, 3, 0)):
        at = pl.multiple_of(((x + d) % NX) * tb, tb)
        loads.append(pltpu.make_async_copy(a_hbm.at[pl.ds(at, tb)], a_v.at[d], ld.at[1 + i]))
    for d in range(NX):
        at = pl.multiple_of(((x + NX - d) % NX) * tb, tb)
        loads.append(pltpu.make_async_copy(g_hbm.at[:, pl.ds(at, tb)], g_v.at[:, pl.ds(d * tb, tb)], ld.at[5 + d]))
    loads.append(pltpu.make_async_copy(m_hbm, m_v, ld.at[9]))
    loads.append(pltpu.make_async_copy(v_hbm, v_v, ld.at[10]))
    loads.append(pltpu.make_async_copy(s_hbm.at[pl.ds(pl.multiple_of(dp * rows, rows), rows)], b_v, ld.at[11]))
    for load in loads[:5]:
        load.start()
    for peer in peers:
        pl.semaphore_signal(barrier, inc=1, device_id=peer, device_id_type=MESH)

    def remote(src, dst, send, recv, to):
        return pltpu.make_async_remote_copy(
            src_ref=src, dst_ref=dst, send_sem=send, recv_sem=recv, device_id=to, device_id_type=MESH
        )

    def span(k):
        return slice(k * kr, (k + 1) * kr)

    def rows_of(k):
        return pl.ds(k * kr, kr)

    def slot(d):
        return pl.ds(d * tb, tb)

    def x_copy(k, d):
        r = rows_of(k)
        return remote(xs.at[d - 1, r], xr.at[d - 1, r], xss.at[k, d - 1], xrs.at[k, d - 1], x_at(d))

    def z_copy(k):
        r = rows_of(k)
        return remote(zs.at[r], zr.at[r], zss.at[k], zrs.at[k], z_far)

    def xa_copy(k, d):
        src, dst = pt.at[k, :, :, :, slot(0)], pt.at[k, :, :, :, slot(d)]
        return remote(src, dst, xas.at[k, d - 1], xar.at[k, d - 1], x_at(d))

    def project(k, d):
        return lax.dot_general(s_v[:, span(k)], a_v[d], (((0,), (1,)), ((), ())), preferred_element_type=f32)

    def send_partial(k):
        first = k == TURN[0]
        if first:
            loads[0].wait()
        for d in (2, 1, 3):
            if first:
                loads[d].wait()
            xs[d - 1, span(k)] = project(k, d).astype(bf16)
            if first and d == 2:
                pl.semaphore_wait(barrier, len(peers))
            x_copy(k, d).start()
        if first:
            for load in loads[5:]:
                load.start()
            loads[4].wait()
        xo[span(k)] = project(k, 0)

    def turn_g():
        for d in range(NX):
            loads[5 + d].wait()
            gt[d * tb : (d + 1) * tb] = g_v[:, d * tb : (d + 1) * tb].T

    def piece1(i):
        k = TURN[i]
        r = span(k)
        for d in (1, 3, 2):
            x_copy(k, d).wait_recv()
        h = xo[r] + xr[0, r].astype(f32) + xr[1, r].astype(f32) + xr[2, r].astype(f32)
        zs[r] = h.astype(bf16)
        z_copy(k).start()
        ho[r] = h

    def piece2(i):
        k = TURN[i]
        r = span(k)
        z_copy(k).wait_recv()
        pt[k, :, :, :, 0:tb] = (ho[r] + zr[r].astype(f32)).astype(bf16).reshape(NY, 2, own, tb)
        for d in (2, 1, 3):
            xa_copy(k, d).start()

    def cols(u):
        return pl.ds(unit[u][2], unit[u][3] - unit[u][2])

    def c_copy(u):
        k = unit[u][0]
        return remote(cs.at[k, :, :, cols(u)], cr.at[k, :, :, cols(u)], css.at[u], crs.at[u], core)

    def y_copy(u, d):
        k = unit[u][0]
        src, dst = ys.at[k, (y + d) % NY, :, cols(u)], yr.at[k, d - 1, :, cols(u)]
        return remote(src, dst, yss.at[u, d - 1], yrs.at[u, d - 1], y_at(d))

    def w_copy(u):
        k, h = unit[u][:2]
        place = (zl - k + NZ - 1) % NZ
        return remote(ws.at[k, :, cols(u)], wr.at[place, :, cols(u)], wss.at[u], wrs.at[h, place], z_at(k))

    def w_wait(u, d):
        k, h = unit[u][:2]
        theirs = wr.at[d - 1, :, cols(u)]
        remote(theirs, theirs, wss.at[u], wrs.at[h, d - 1], z_at((k + d) % NZ)).wait_recv()

    def b_copy(u, d):
        k, h = unit[u][:2]
        mine = lr.at[k, y, c, :, cols(u)]
        return remote(mine, mine, bss.at[h, d - 1], brs.at[u], z_at((k + d) % NZ))

    def ya_copy(u, d):
        mine = lr.at[unit[u][0], y, c, :, cols(u)]
        return remote(mine, mine, yas.at[u, d - 1], yar.at[u, d - 1], y_at(d))

    def ya_wait(u, d):
        theirs = lr.at[unit[u][0], (y + NY - d) % NY, c, :, cols(u)]
        remote(theirs, theirs, yas.at[u, d - 1], yar.at[u, d - 1], y_at(d)).wait_recv()

    def c2_copy(u, d):
        mine = lr.at[unit[u][0], (y + NY - d) % NY, c, :, cols(u)]
        return remote(mine, mine, c2s.at[u, d], c2r.at[u, d], core)

    def c2_wait(u, d):
        theirs = lr.at[unit[u][0], (y + NY - d) % NY, 1 - c, :, cols(u)]
        remote(theirs, theirs, c2s.at[u, d], c2r.at[u, d], core).wait_recv()

    def unit0(u):
        k, h, lo, hi = unit[u]
        if h == 0:
            for d in (1, 3, 2):
                xa_copy(k, d).wait_recv()

        def product(parity):
            p = pt[k, :, parity].reshape(NY * own, pt.shape[-1])
            return jnp.dot(p, gt[:, lo:hi], preferred_element_type=f32).reshape(NY, own, hi - lo)

        cs[k, :, :, lo:hi] = product(1 - c).astype(bf16)
        c_copy(u).start()
        rf[k, :, :, lo:hi] = product(c)

    def unit1(u):
        k, h, lo, hi = unit[u]
        c_copy(u).wait_recv()
        for d in (2, 1, 3, 0):
            yy = (y + d) % NY
            both = rf[k, yy, :, lo:hi] + cr[k, yy, :, lo:hi].astype(f32)
            if d:
                ys[k, yy, :, lo:hi] = both.astype(bf16)
                y_copy(u, d).start()
            else:
                ty[k, :, lo:hi] = both

    def unit2(u):
        k, h, lo, hi = unit[u]
        for d in (1, 3, 2):
            y_copy(u, d).wait_recv()
        total = ty[k, :, lo:hi]
        for d in (1, 2, 3):
            total = total + yr[k, d - 1, :, lo:hi].astype(f32)
        ty[k, :, lo:hi] = total

        @pl.when(zl != k)
        def _():
            ws[k, :, lo:hi] = total.astype(bf16)
            w_copy(u).start()

        if h == 0:
            sent_first(k)

    def sent_first(k):
        for d in (1, 2, 3):
            x_copy(k, d).wait_send()
            xa_copy(k, d).wait_send()
        z_copy(k).wait_send()

    def sent_sums(u):
        c_copy(u).wait_send()
        for d in (1, 2, 3):
            y_copy(u, d).wait_send()

        @pl.when(zl != unit[u][0])
        def _():
            w_copy(u).wait_send()

    def sent_steps(u):
        @pl.when(zl == unit[u][0])
        def _():
            for d in (1, 2, 3):
                b_copy(u, d).wait_send()

    def sent_gathered(u):
        for d in (1, 2, 3):
            ya_copy(u, d).wait_send()
        for d in range(NY):
            c2_copy(u, d).wait_send()

    def far_first(k):
        return sorted((1, 2, 3), key=lambda d: -abs((k + d) % NZ - k))

    def unit3(u):
        k, h, lo, hi = unit[u]

        @pl.when(zl == k)
        def _():
            for d in (1, 2, 3):
                w_wait(u, d)
            if h == 0:
                loads[9].wait()
                loads[10].wait()
            reduced = ty[k, :, lo:hi]
            for d in (1, 2, 3):
                reduced = reduced + wr[d - 1, :, lo:hi].astype(f32)
            first, second = m_v[:, lo:hi], v_v[:, lo:hi]
            first_hat = (0.9 / (1.0 - 0.9**STEP)) * first + (0.1 / (1.0 - 0.9**STEP)) * reduced
            second_hat = (0.999 / (1.0 - 0.999**STEP)) * second + (0.001 / (1.0 - 0.999**STEP)) * reduced * reduced
            lr[k, y, c, :, lo:hi] = (first_hat / (jnp.sqrt(second_hat) + 1e-08)).astype(bf16)
            for d in far_first(k):
                b_copy(u, d).start()
            nf_v[:, lo:hi] = 0.9 * first + 0.1 * reduced
            ns_v[:, lo:hi] = 0.999 * second + 0.001 * reduced * reduced

    def unit4(u):
        @pl.when(zl != unit[u][0])
        def _():
            b_copy(u, 1).wait_recv()

        for d in (2, 1, 3):
            ya_copy(u, d).start()
        c2_copy(u, 0).start()
        sent_sums(u)

    def unit5(u):
        for d in (1, 3, 2):
            ya_wait(u, d)
            c2_copy(u, d).start()
        sent_steps(u)

    def unit6(u):
        k, h, lo, hi = unit[u]
        for d in (0, 1, 3, 2):
            c2_wait(u, d)
        if u == 0:
            loads[11].wait()
        low = lr[k, :, :, :, lo:hi].reshape(kr, hi - lo)
        part = lax.dot_general(
            low, b_v[:, k * kr : (k + 1) * kr], (((0,), (1,)), ((), ())), preferred_element_type=f32
        )
        if k == TURN[0]:
            acc[lo:hi] = part
        elif k != TURN[-1]:
            acc[lo:hi] += part
        else:
            up_v[lo:hi] = (acc[lo:hi] + part).astype(bf16)
        sent_gathered(u)

    for k in TURN:
        send_partial(k)
    turn_g()
    stages = dict(P=(None, piece1, piece2), U=(unit0, unit1, unit2, unit3, unit4, unit5, unit6))
    for name in ORDER:
        stages[name[0]][int(name[1])](int(name[2]))


def hand_on(up_in, nf_in, ns_in, up_out, nf_out, ns_out, sem):
    pairs = ((up_in, up_out), (nf_in, nf_out), (ns_in, ns_out))
    writes = [pltpu.make_async_copy(src, dst, sem.at[i]) for i, (src, dst) in enumerate(pairs)]
    for write in writes:
        write.start()
    for write in writes:
        write.wait()


def local(activations, grad_out, subspace, first_moment, second_moment):
    tokens, depth = activations.shape
    ff = grad_out.shape[1]
    rank = subspace.shape[1]
    own = first_moment.shape[0]
    rows = subspace.shape[0] // lax.axis_size("dp")
    tb = tokens // NX
    kr = rank // KC
    f32, bf16 = jnp.float32, jnp.bfloat16
    dma = pltpu.SemaphoreType.DMA
    anywhere = pl.BlockSpec(memory_space=pl.ANY)
    scratch = [
        ((NX, tb, depth), bf16),
        ((ff, tokens), bf16),
        ((tokens, ff), bf16),
        ((depth, rank), bf16),
        ((rows, rank), bf16),
        ((own, ff), f32),
        ((own, ff), f32),
        ((NX - 1, rank, tb), bf16),
        ((rank, tb), f32),
        ((NX - 1, rank, tb), bf16),
        ((rank, tb), f32),
        ((rank, tb), bf16),
        ((rank, tb), bf16),
        ((KC, NY, 2, own, tokens), bf16),
        ((KC, NY, own, ff), f32),
        ((KC, NY, own, ff), bf16),
        ((KC, NY, own, ff), bf16),
        ((KC, own, ff), f32),
        ((KC, NY, own, ff), bf16),
        ((KC, NY - 1, own, ff), bf16),
        ((KC, own, ff), bf16),
        ((NZ - 1, own, ff), bf16),
        ((KC, NY, 2, own, ff), bf16),
        ((ff, rows), f32),
    ]
    nu, nh = len(units(ff)), max(CUTS)
    sems = [(12,), (KC, 3), (KC, 3), (KC,), (KC,), (KC, 3), (KC, 3)]
    sems += [(nu,), (nu,), (nu, 3), (nu, 3), (nu,), (nh, 3), (nh, 3), (nu,), (nu, 3), (nu, 3), (nu, NY), (nu, NY)]
    flops = 2 * tokens * rank * (depth + ff) + 2 * rows * rank * ff
    shapes = (
        jax.ShapeDtypeStruct((ff, rows), bf16),
        jax.ShapeDtypeStruct((own, ff), f32),
        jax.ShapeDtypeStruct((own, ff), f32),
    )
    made = pl.pallas_call(
        kernel,
        out_shape=tuple(pltpu.VMEM(out.shape, out.dtype) for out in shapes),
        in_specs=[anywhere] * 5,
        out_specs=(pl.BlockSpec(memory_space=pltpu.VMEM),) * 3,
        scratch_shapes=[pltpu.VMEM(shape, dtype) for shape, dtype in scratch] + [dma(shape) for shape in sems],
        compiler_params=pltpu.CompilerParams(collective_id=0, has_side_effects=True, vmem_limit_bytes=56 << 20),
        cost_estimate=pl.CostEstimate(flops=flops, bytes_accessed=8 << 20, transcendentals=own * ff),
        name="galore",
    )(activations, grad_out.T, subspace, first_moment, second_moment)
    update, new_first, new_second = pl.pallas_call(
        hand_on,
        out_shape=shapes,
        in_specs=[anywhere] * 3,
        out_specs=(anywhere,) * 3,
        scratch_shapes=[dma((3,))],
        name="hand_on",
    )(*[pltpu.with_memory_space_constraint(one, pltpu.VMEM) for one in made])
    return update.T, new_first, new_second


def solution(mesh):
    in_specs = (P("dp", "tensor"), P("dp", "tensor"), P(), P("dp", "tensor"), P("dp", "tensor"))
    out_specs = (P("dp", "tensor"), P("dp", "tensor"), P("dp", "tensor"))
    return jax.shard_map(local, mesh=mesh, in_specs=in_specs, out_specs=out_specs, check_vma=False)
```
